32 devices in a mesh: orb: 8 (over y, x, core), ao: 4 (over z).
Axes of the slice: x: 2, y: 2, z: 4, core: 2. Of those that a mesh axis runs over, the one named last changes fastest.
Arguments:
- coeff: float32 [2, 8, 64, 80, 128], P(None, 'orb', 'ao')
- metric_coeff: float32 [2, 8, 64, 80, 128], P(None, 'orb', 'ao')
- tile_list: int32 [2, 8, 64], P(None, 'orb', 'ao'), may hold values from 0 to 191, as said below
- tile_atoms: int32 [192, 128], replicated, may hold values from 0 to 7, never falling along the last dimension, each value on 1 to 32 neighbouring positions
Outputs:
- coeff_out: float32 [2, 8, 64, 80, 128], P(None, 'orb', 'ao')
- metric_out: float32 [2, 8, 64, 80, 128], P(None, 'orb', 'ao')
The draws below stay inside these ranges and needn't reach their ends.
Inputs may be any that keep to these rules, and one draw needn't show every extreme that they name: `tile_list`: within one block the ids are distinct, and an id at list position k leaves the remainder k // 16 when divided by 4. `tile_atoms`: along a tile's atomic orbitals the slot never falls, and each of the 8 slots holds 1 to 32 atomic orbitals.
All inputs are finite; a program needn't handle non-finite values.
Results may differ from the reference program's by a relative error of at most 0.0003.
Values sent between devices are 32-bit elements; how exact they have to be, the bound alone decides.
No kernel may reach another device: no remote copies, remote signals or barrier semaphores. Data moves between devices by JAX's collectives and lax.ppermute only.
A program may use at most 64 MiB of HBM per device.

```python
import math
import jax
import jax.numpy as jnp
import numpy as np
from jax import lax

BLOCK = 80
TILE_AO = 128
LIST = 64
ATOMS = 8
ROUNDS = 2
LIST_DEV = 16
GROUPS = 8
TILES = 192


def shared_field(key, spread):
    field_shape = (2, GROUPS, LIST, BLOCK, TILE_AO)
    normal_key = jax.random.fold_in(key, 0)
    orbital_key = jax.random.fold_in(key, 2)
    atomic_key = jax.random.fold_in(key, 3)
    normal_part = jax.random.normal(normal_key, field_shape, jnp.float32)
    orbital_scale = jnp.exp(jax.random.uniform(orbital_key, (2, GROUPS, 1, BLOCK, 1), jnp.float32, -spread, spread))
    atomic_scale = jnp.exp(jax.random.uniform(atomic_key, (2, GROUPS, LIST, 1, TILE_AO), jnp.float32, -spread, spread))
    group_scale = 1.0 + 0.5 * jnp.arange(GROUPS, dtype=jnp.float32).reshape(1, GROUPS, 1, 1, 1) / GROUPS
    return (normal_part, 0.5 * orbital_scale * atomic_scale * group_scale)


def draw_coeff(key, part):
    normal_part, scales = shared_field(key, 0.7)
    values = normal_part * scales
    return values.astype(jnp.float32)


def draw_metric_coeff(key, part):
    normal_part, scales = shared_field(key, 0.7)
    key = jax.random.fold_in(key, 5)
    noise = jax.random.normal(key, normal_part.shape, jnp.float32)
    values = (normal_part + 0.4 * noise) * scales
    return values.astype(jnp.float32)


def draw_tile_list(key, part):
    key = jax.random.fold_in(key, 7)
    start_key, score_key = jax.random.split(key)
    shards = LIST // LIST_DEV
    window = 2 * LIST_DEV
    starts = jax.random.randint(start_key, (2, GROUPS, 1, 1), 0, LIST_DEV + 1)
    slot_index = jnp.arange(2).reshape(2, 1, 1, 1)
    group_index = jnp.arange(GROUPS).reshape(1, GROUPS, 1, 1)
    starts = jnp.where((slot_index == 0) & (group_index == 0), 0, starts)
    starts = jnp.where((slot_index == 1) & (group_index == 0), LIST_DEV, starts)
    offsets = jnp.arange(window).reshape(1, 1, 1, window)
    shard_index = jnp.arange(shards).reshape(1, 1, shards, 1)
    scores = jax.random.randint(score_key, (2, GROUPS, shards, window), 0, 1 << 20) * window + offsets
    first_pick = (slot_index == 0) & (group_index == 0) & (offsets == 0) & (shard_index == 0)
    last_pick = (slot_index == 1) & (group_index == 0) & (offsets == window - 1) & (shard_index == shards - 1)
    scores = jnp.where(first_pick | last_pick, -1, scores)
    chosen = jnp.argsort(scores, axis=-1)[..., :LIST_DEV]
    tile_ids = (starts + chosen) * shards + shard_index
    return tile_ids.reshape(2, GROUPS, LIST).astype(jnp.int32)


def profile(count, total, bound, slope):
    weights = [(1 << 20) // math.isqrt(rank ** slope) + 1 for rank in range(2, count + 1)]
    spare, counts = total - bound - (count - 1), [1] * (count - 1)
    while spare > 0:
        candidates = [i for i in range(count - 1) if counts[i] < bound]
        pool, remaining = sum([weights[i] for i in candidates]), spare
        for i in candidates:
            more = min(bound - counts[i], max(1, remaining * weights[i] // pool), spare)
            counts[i] = counts[i] + more
            spare = spare - more
    return np.array([bound] + counts)


def ragged_sizes(key, count, total, reach, skew):
    if count == 2:
        one = jax.random.randint(key, (), max(1, total - reach), min(reach, total - 1) + 1)
        return jnp.stack([one, total - one])
    lengths = jnp.asarray(profile(count, total, reach, skew), jnp.int32)
    couples = (count - 1) // 2
    giver, receiver = lengths[1:1 + 2 * couples:2], lengths[2:2 + 2 * couples:2]
    room = jnp.minimum(giver - 1, reach - receiver)
    passed = jax.random.randint(jax.random.fold_in(key, 1), (couples,), 0, 1 << 20) % (room + 1)
    lengths = lengths.at[1:1 + 2 * couples:2].set(giver - passed).at[2:2 + 2 * couples:2].set(receiver + passed)
    return lengths[jax.random.permutation(jax.random.fold_in(key, 2), count)]


def setup_inputs(seed: int = 0) -> dict:
    splits = jax.random.split(jax.random.key(seed), 5)
    return {
        "coeff": draw_coeff(jax.random.fold_in(splits[4], 71), 0),
        "metric_coeff": draw_metric_coeff(jax.random.fold_in(splits[4], 71), 0),
        "tile_list": draw_tile_list(jax.random.fold_in(splits[4], 71), 0),
        "tile_atoms": jax.vmap(lambda own: jnp.searchsorted(jnp.cumsum(ragged_sizes(own, ATOMS, TILE_AO, TILE_AO // 4, 2)), jnp.arange(TILE_AO), side="right"))(jax.random.split(splits[3], TILES)).reshape((TILES, TILE_AO)).astype(jnp.int32),
    }


STEP_LENGTH = 3.0
EPSILON = 1e-12
EXACT_MODE = lax.Precision.HIGHEST

def charge_half(stacked, atom_rows, weight):
    coeffs = stacked[0]
    metric_part = stacked[1]
    member = (atom_rows[:, None, :] == jnp.arange(ATOMS, dtype=jnp.int32)[None, :, None]).astype(jnp.float32)
    charges = jnp.einsum('tsa,tia->tsi', member, coeffs * metric_part, precision=EXACT_MODE)
    spread = jnp.einsum('tsa,tsi->tia', member, charges, precision=EXACT_MODE) * weight[:, None, None]
    first_term = jnp.einsum('tia,tja->ij', coeffs * spread, metric_part, precision=EXACT_MODE)
    second_term = jnp.einsum('tia,tja->ij', metric_part * spread, coeffs, precision=EXACT_MODE)
    return 0.5 * (first_term + second_term)

def extended(top_block, low_block, top_tiles, low_tiles, tile_atoms):
    matches = (top_tiles[:, None] == low_tiles[None, :]).astype(jnp.float32)
    on_top = jnp.concatenate([top_block, jnp.einsum('kl,clba->ckba', matches, low_block, precision=EXACT_MODE)], axis=2)
    on_low = jnp.concatenate([jnp.einsum('kl,ckba->clba', matches, top_block, precision=EXACT_MODE), low_block], axis=2)
    unshared = 1.0 - lax.optimization_barrier(jnp.sum(matches, axis=0))
    halves = charge_half(on_top, jnp.take(tile_atoms, top_tiles, axis=0), jnp.ones_like(unshared))
    halves = halves + charge_half(on_low, jnp.take(tile_atoms, low_tiles, axis=0), unshared)
    return (on_top, on_low, halves)

def cayley(gradient, step_scale):
    generator = step_scale * gradient
    identity = jnp.eye(gradient.shape[0], dtype=gradient.dtype)
    raised = identity + 0.5 * generator
    metric = identity - 0.25 * jnp.dot(generator, generator, precision=EXACT_MODE)
    factor = jnp.linalg.cholesky(metric)
    return jax.scipy.linalg.cho_solve((factor, True), jnp.dot(raised, raised, precision=EXACT_MODE))

def rotate(columns, stacked):
    return jnp.einsum('ij,ctia->ctja', columns, stacked, precision=EXACT_MODE)

def group_gradient(packed, tile_atoms):
    halves = extended(packed[0], packed[1], packed[2], packed[3], tile_atoms)[2]
    return 4.0 * (halves - halves.T)

def reference(coeff, metric_coeff, tile_list, tile_atoms):
    top_block = jnp.stack([coeff[0], metric_coeff[0]], axis=1)
    low_block = jnp.stack([coeff[1], metric_coeff[1]], axis=1)
    top_tiles = tile_list[0]
    low_tiles = tile_list[1]
    for round_index in range(ROUNDS):
        packed_all = (top_block, low_block, top_tiles, low_tiles)
        gradients = lax.map(lambda packed: group_gradient(packed, tile_atoms), packed_all)
        step_scale = STEP_LENGTH / jnp.sqrt(jnp.sum(gradients * gradients) / GROUPS + EPSILON)

        def turned(packed):
            on_top, on_low, halves = extended(packed[0], packed[1], packed[2], packed[3], tile_atoms)
            rotation = cayley(4.0 * (halves - halves.T), step_scale)
            return (rotate(rotation[:, :BLOCK], on_top), rotate(rotation[:, BLOCK:], on_low))
        top_block, low_block = lax.map(turned, packed_all)
        if round_index + 1 < ROUNDS:
            top_block, low_block = (jnp.concatenate([top_block[:1], low_block[:1], top_block[1:-1]]), jnp.concatenate([low_block[1:], top_block[-1:]]))
            top_tiles, low_tiles = (jnp.concatenate([top_tiles[:1], low_tiles[:1], top_tiles[1:-1]]), jnp.concatenate([low_tiles[1:], top_tiles[-1:]]))
    return (jnp.stack([top_block[:, 0], low_block[:, 0]]), jnp.stack([top_block[:, 1], low_block[:, 1]]))
```

```python
import functools

import jax
import jax.numpy as jnp
from jax import lax
from jax.experimental import pallas as pl
from jax.experimental.pallas import tpu as pltpu
from jax.sharding import PartitionSpec as P

ATOMS = 8
LANES = 128
STEP_LENGTH = 3.0
EPSILON = 1e-12
CONVERGED = 1.2e-7
SOME_VMEM = 20_000_000

F32 = jnp.float32
BF16 = jnp.bfloat16
NT = (((1,), (1,)), ((), ()))
NN = (((1,), (0,)), ((), ()))
HBM = pl.BlockSpec(memory_space=pltpu.HBM)
VMEM = pl.BlockSpec(memory_space=pltpu.VMEM)


def halves(value):
    high = value.astype(BF16)
    return high, (value - high.astype(F32)).astype(BF16)


def dot(left, right, dims):
    return lax.dot_general(left, right, dims, preferred_element_type=F32)


def stacked_dot(left, right, rows, dims):
    wide = dot(left, right[0], dims)
    return wide[:rows] + (wide[rows:] + dot(left[:rows], right[1], dims))


def packed_rows(orbitals):
    pieces = -(-orbitals // (LANES - orbitals))
    tail = 2 * orbitals // (pieces + 1) // 8 * 8
    return 2 * orbitals - tail, tail, pieces


def pack(value, orbitals):
    keep, tail, pieces = packed_rows(orbitals)
    spare = LANES - orbitals
    lane = lax.broadcasted_iota(jnp.int32, (tail, LANES), 1)
    moved = [
        jnp.where(lane >= orbitals, pltpu.roll(value[keep:], (orbitals - i * spare) % LANES, 1), 0.0)
        for i in range(pieces)
    ]
    if keep > pieces * tail:
        moved.append(jnp.zeros((keep - pieces * tail, LANES), F32))
    return value[:keep] + jnp.concatenate(moved, axis=0)


def unpack(value, orbitals):
    keep, tail, pieces = packed_rows(orbitals)
    spare = LANES - orbitals
    lane = lax.broadcasted_iota(jnp.int32, (keep, LANES), 1)
    moved = jnp.where(lane >= orbitals, value, 0.0)
    last = sum(
        pltpu.roll(moved[i * tail : (i + 1) * tail], (i * spare - orbitals) % LANES, 1) for i in range(pieces)
    )
    return jnp.concatenate([jnp.where(lane < orbitals, value, 0.0), last], axis=0)


def crosses(position, last):
    return ((position % 4 == 3) & (position < last)) | ((position % 4 == 0) & (position > 0))


class Blocks:
    def __init__(self, first_round, refs, buffer, lists, sems, count, orbitals):
        self.count, self.orbitals, self.buffer, self.lists, self.sems = count, orbitals, buffer, lists, sems
        self.first_round, self.refs = first_round, refs

    def copy(self, slot, part, source):
        target = self.lists.at[slot] if part == 2 else self.buffer.at[slot, part]
        return pltpu.make_async_copy(source, target, self.sems.at[slot, part])

    def start(self):
        rows = self.count * self.orbitals
        if self.first_round:
            tile_list, coeff, metric = self.refs
            for slot in (1, 0):
                for part, source in ((2, tile_list), (0, coeff), (1, metric)):
                    self.copy(slot, part, source.at[slot]).start()
            return
        own_coeff, own_metric, even, odd_metric, relayed, rebuilt = self.refs
        position, last = lax.axis_index("orb"), lax.axis_size("orb") - 1
        odd = position % 2 == 1
        across = crosses(position, last)

        def begin(condition, slot, coeff, metric, metric_row):
            note_row = 2 * rows if metric_row else rows

            @pl.when(condition)
            def _():
                self.copy(slot, 2, coeff.at[pl.ds(note_row, 8)]).start()
                self.copy(slot, 0, coeff.at[pl.ds(0, rows)]).start()
                self.copy(slot, 1, metric.at[pl.ds(metric_row, rows)]).start()

        for slot, from_even, end in ((1, jnp.logical_not(odd), last), (0, odd, 0)):
            from_odd = jnp.logical_not(from_even) & (position != end)
            begin(from_even, slot, even, even, rows)
            begin(position == end, slot, own_coeff, own_metric, 0)
            begin(from_odd & across, slot, relayed, odd_metric, 0)
            begin(from_odd & jnp.logical_not(across), slot, rebuilt, odd_metric, 0)

    def wait(self, slot):
        for part in (2, 0, 1):
            if self.first_round:
                source = self.refs[0 if part == 2 else 1].at[slot]
            else:
                source = self.refs[0].at[pl.ds(0, 8 if part == 2 else self.count * self.orbitals)]
            self.copy(slot, part, source).wait()

    def tile(self, slot, k):
        return self.lists[slot, 0, k].astype(jnp.int32)

    def value(self, slot, c, k):
        return self.buffer[slot, c, k * self.orbitals : (k + 1) * self.orbitals, :]

    def wide(self, slot, c, k):
        return jnp.concatenate([self.value(slot, c, k), self.value(slot, c, k + 1)], axis=1)

    def place(self, slot, k):
        entry, place = self.tile(slot, k), jnp.int32(self.count)
        for l in range(self.count):
            place = jnp.where(entry == self.tile(1 - slot, l), jnp.int32(l), place)
        return place


def own_rows(slot, orbitals):
    return slice(slot * orbitals, (slot + 1) * orbitals)


def lanes_at(k, tiles=1):
    if isinstance(k, int):
        return slice(k * LANES, (k + tiles) * LANES)
    return pl.ds(pl.multiple_of(k * LANES, LANES), tiles * LANES)


def clear_spare(slot, blocks, arrays):
    for array in arrays:
        for c in range(2):
            array[slot, c, own_rows(slot, blocks.orbitals), blocks.count * LANES :] = jnp.zeros(
                (blocks.orbitals, LANES), BF16
            )


def carry(blocks, arrays):
    for slot in range(2):
        rows = own_rows(1 - slot, blocks.orbitals)
        for k in range(blocks.count):
            here, there = lanes_at(k), lanes_at(blocks.place(slot, k))
            for array in arrays:
                for c in range(2):
                    array[slot, c, rows, here] = array[1 - slot, c, rows, there]


def gradient_kernel(first_round, count, orbitals, sources, atoms_hbm, *refs):
    inputs, refs = refs[:sources], refs[sources:]
    out_ref, right_high, right_rest, buffer, lists, sems, atoms_ref, atoms_sem, left = refs
    blocks = Blocks(first_round, inputs, buffer, lists, sems, count, orbitals)
    atoms_copy = pltpu.make_async_copy(atoms_hbm, atoms_ref, atoms_sem)
    atoms_copy.start()
    blocks.start()
    width, gap = count * LANES, LANES - orbitals
    chunk = min(8, count)
    slots = lax.broadcasted_iota(jnp.int32, (ATOMS, LANES), 0)
    blank = jnp.zeros((ATOMS, LANES), F32)
    lane = lax.broadcasted_iota(jnp.int32, (orbitals, count * ATOMS), 1) // (2 * ATOMS)
    atoms_copy.wait()

    for slot in (1, 0):
        blocks.wait(slot)
        clear_spare(slot, blocks, (right_high, right_rest))
        rows = own_rows(slot, orbitals)
        member = []
        for k in range(count):
            one = (atoms_ref[pl.ds(blocks.tile(slot, k), 1), :] == slots).astype(F32)
            member.append(jnp.concatenate([blank, one] if k % 2 else [one, blank], axis=1))
        member = jnp.concatenate(member, axis=0).astype(BF16)
        member_wide = jnp.concatenate([member, member], axis=1)
        member_tall = jnp.concatenate([member, member], axis=0)

        for first in range(0, count, chunk):
            pairs = range(0, chunk, 2)
            coeffs = jnp.concatenate([blocks.wide(slot, 0, first + k) for k in pairs], axis=0)
            metric = jnp.concatenate([blocks.wide(slot, 1, first + k) for k in pairs], axis=0)
            charges = dot(jnp.concatenate(halves(coeffs * metric), axis=1), member_wide, NT)
            charges = jnp.concatenate(
                [
                    jnp.where(lane == first // 2 + j, charges[j * orbitals : (j + 1) * orbitals], 0.0)
                    for j in range(len(pairs))
                ],
                axis=0,
            )
            spread = dot(jnp.concatenate(halves(charges), axis=1), member_tall, NN)
            for c, value in enumerate((coeffs, metric)):
                weighted, plain = halves(value * spread), halves(value)
                for j, k in enumerate(pairs):
                    picked, here = slice(j * orbitals, (j + 1) * orbitals), lanes_at(first + k, 2)
                    left[slot, c, :orbitals, here] = weighted[0][picked]
                    left[slot, c, orbitals:, here] = weighted[1][picked]
                    right_high[slot, c, rows, here] = plain[0][picked]
                    right_rest[slot, c, rows, here] = plain[1][picked]


    carry(blocks, (right_high, right_rest))
    fill_lanes = jnp.zeros((2 * orbitals, gap), F32)
    fill_rows = jnp.zeros((gap, LANES), F32)
    products = []
    for slot in range(2):
        wide = sum(dot(right_high[slot, 1 - c, :, :width], left[slot, c], NT) for c in range(2))
        rest = sum(dot(right_rest[slot, 1 - c, :, :width], left[slot, c, :orbitals], NT) for c in range(2))
        value = jnp.concatenate([wide[:, :orbitals] + (wide[:, orbitals:] + rest), fill_lanes], axis=1)
        products.append(
            [jnp.concatenate([value[own_rows(i, orbitals)], fill_rows], axis=0) for i in range(2)]
        )
    (upper, upper_lower), (lower_upper, lower) = products
    row = lax.broadcasted_iota(jnp.int32, (LANES, LANES), 0)
    column = lax.broadcasted_iota(jnp.int32, (LANES, LANES), 1)
    diagonal = jnp.where(column > row, upper.T - upper, jnp.where(column < row, lower.T - lower, 0.0))
    cross = upper_lower.T - lower_upper
    packed = pack(jnp.concatenate([2.0 * diagonal[:orbitals], 2.0 * cross[:orbitals]], axis=0), orbitals)
    for z in range(out_ref.shape[0]):
        out_ref[z] = packed

def norm_kernel(parts_ref, packed_ref, norm_ref):
    packed = parts_ref[0]
    for z in range(1, parts_ref.shape[0]):
        packed = packed + parts_ref[z]
    packed_ref[...] = packed
    total = jnp.broadcast_to(2.0 * jnp.sum(packed * packed, keepdims=True), norm_ref.shape[1:])
    for g in range(norm_ref.shape[0]):
        norm_ref[g] = total


def compact(turn, orbitals):
    lane = lax.broadcasted_iota(jnp.int32, turn.shape, 1)
    turn = jnp.where(lane < LANES, turn, 0.0) + pltpu.roll(
        jnp.where(lane >= LANES, turn, 0.0), LANES + orbitals, 1
    )
    return halves(turn[:, : 2 * orbitals])


def later_slot(position):
    return jnp.where((position % 2 == 0) & (position != 0), 0, 1)


def note_of(tile, count):
    lane = lax.broadcasted_iota(jnp.int32, (8, LANES), 1)
    ids = jnp.zeros((8, LANES), jnp.int32)
    for k in range(count):
        ids = jnp.where(lane == k, tile(k), ids)
    return ids.astype(F32)


def apply(turn_ref, slot, c, data_high, data_rest, count, orbitals, put):
    chunk = min(4, count)
    for first in range(0, count, chunk):
        here = lanes_at(first, chunk)
        value = stacked_dot(
            turn_ref[slot], (data_high[slot, c, :, here], data_rest[slot, c, :, here]), orbitals, NN
        )
        for j in range(chunk):
            put(slice((first + j) * orbitals, (first + j + 1) * orbitals), value[:, lanes_at(j)])


def later_kernel(count, orbitals, turn_ref, data_high, data_rest, list_hbm, out_ref, lists, list_sem):
    rows = count * orbitals
    list_copy = pltpu.make_async_copy(list_hbm, lists, list_sem)
    list_copy.start()
    slot = later_slot(lax.axis_index("orb"))
    for c in range(2):

        def put(place, value, c=c):
            out_ref[c * rows + place.start : c * rows + place.stop, :] = value

        apply(turn_ref, slot, c, data_high, data_rest, count, orbitals, put)
    list_copy.wait()
    out_ref[2 * rows :] = note_of(lambda k: lists[slot, 0, k], count)


def rotation_kernel(first_round, count, orbitals, groups, *refs):
    norm_ref, packed_ref, data_high, data_rest = refs[:4]
    final = not first_round
    if first_round:
        list_hbm, odd_coeff, odd_metric, rows_ref, turn_ref, lists, list_sem, power_ref, total_ref = refs[4:]
        list_copy = pltpu.make_async_copy(list_hbm, lists, list_sem)
        list_copy.start()
    else:
        outs, (result, out_sems, power_ref, total_ref, turn_ref) = refs[4:6], refs[6:]
    size, wide, gap = 2 * orbitals, 2 * LANES, LANES - orbitals
    rows = count * orbitals

    squares = norm_ref[0]
    for g in range(1, groups):
        squares = squares + norm_ref[g]
    scale = (STEP_LENGTH / jnp.sqrt(squares / groups + EPSILON))[:1, :]
    row = lax.broadcasted_iota(jnp.int32, (LANES, LANES), 0)
    column = lax.broadcasted_iota(jnp.int32, (LANES, LANES), 1)
    fill = jnp.zeros((gap, LANES), F32)
    scaled = unpack(packed_ref[...], orbitals) * (-0.5 * scale)
    diagonal = jnp.concatenate([scaled[:orbitals], fill], axis=0)
    cross = jnp.concatenate([scaled[orbitals:], fill], axis=0)
    above = jnp.where(column > row, diagonal, 0.0)
    below = jnp.where(column < row, diagonal, 0.0)
    generator = jnp.concatenate(
        [
            jnp.concatenate([(above - above.T)[:orbitals], cross[:orbitals]], axis=1),
            jnp.concatenate([-cross.T[:orbitals], (below - below.T)[:orbitals]], axis=1),
        ],
        axis=0,
    )
    big_row = lax.broadcasted_iota(jnp.int32, (size, wide), 0)
    big_column = lax.broadcasted_iota(jnp.int32, (size, wide), 1)
    identity = (big_column == jnp.where(big_row < orbitals, big_row, big_row + gap)).astype(F32)

    def spaced(value):
        blank = jnp.zeros((gap, wide), value.dtype)
        return jnp.concatenate([value[:orbitals], blank, value[orbitals:], blank], axis=0)

    def times(left, right):
        high, rest = halves(right)
        return stacked_dot(
            jnp.concatenate(halves(left), axis=0), (spaced(high), spaced(rest)), left.shape[0], NN
        )

    square = -times(generator, generator)
    bound = jnp.sqrt(0.5 * jnp.sum(square * square, keepdims=True))
    centre = 1.0 + 0.5 * bound
    radius = 0.5 * bound / centre
    power_ref[...] = radius * identity - square * (1.0 / centre)
    total_ref[...] = identity + generator

    def more(radius):
        power, total = power_ref[...], total_ref[...]
        product = times(jnp.concatenate([total, power], axis=0), power)
        total_ref[...] = total + product[:size]
        power_ref[...] = product[size:]
        return radius * radius

    lax.while_loop(lambda radius: radius > CONVERGED, more, jnp.max(radius))
    turn = total_ref[...] * (2.0 / centre) - identity
    turn_high, turn_rest = compact(turn, orbitals)
    for slot in range(2):
        mine = own_rows(slot, orbitals)
        turn_ref[slot, :orbitals] = turn_high[mine]
        turn_ref[slot, orbitals:] = turn_rest[mine]

    if final:
        stores = []
        for slot in range(2):
            for c in range(2):

                def put(place, value, slot=slot, c=c):
                    result[slot, c, place, :] = value

                apply(turn_ref, slot, c, data_high, data_rest, count, orbitals, put)
                stores.append(
                    pltpu.make_async_copy(result.at[slot, c], outs[c].at[slot], out_sems.at[slot, c])
                )
                stores[-1].start()
        for copy in stores:
            copy.wait()
        return
    slot = 1 - later_slot(lax.axis_index("orb"))
    total_ref[...] = turn
    odd_rows = pl.ds(pl.multiple_of(slot * orbitals, 8), orbitals)
    rows_ref[8 : 8 + orbitals] = total_ref[odd_rows, :LANES]
    rows_ref[8 + orbitals :] = total_ref[odd_rows, LANES:]
    list_copy.wait()
    row = lax.broadcasted_iota(jnp.int32, (8, LANES), 0)
    notes = [note_of(lambda k, i=i: lists[i, 0, k], count) for i in range(2)]
    rows_ref[:8] = jnp.where(row == 0, notes[0], notes[1])
    odd_coeff[rows:] = jnp.where(slot == 0, notes[0], notes[1])
    for c, out_ref in enumerate((odd_coeff, odd_metric)):

        def put(place, value, out_ref=out_ref):
            out_ref[place, :] = value

        apply(turn_ref, slot, c, data_high, data_rest, count, orbitals, put)


def crossing_kernel(count, orbitals, raw_hbm, turn_hbm, out_ref, *refs):
    buffer, lists, turn_ref, note, result, sems, out_sems = refs[:7]
    data_high, data_rest, other_high, other_rest = refs[7:]
    position, last = lax.axis_index("orb"), lax.axis_size("orb") - 1
    rows, width = count * orbitals, count * LANES

    @pl.when(((position % 4 == 1) & (position < last)) | (position % 4 == 2))
    def _():
        wanted = position % 2
        loads = [pltpu.make_async_copy(turn_hbm.at[pl.ds(0, 8)], lists, sems.at[0, 0])]
        for i, block in enumerate((wanted, 1 - wanted)):
            first = pl.multiple_of(8 + block * orbitals, 8)
            loads.append(pltpu.make_async_copy(raw_hbm.at[block], buffer.at[i], sems.at[i, 1]))
            loads.append(
                pltpu.make_async_copy(turn_hbm.at[pl.ds(first, orbitals)], turn_ref.at[i], sems.at[i, 2])
            )
        for copy in loads:
            copy.start()
        for copy in loads:
            copy.wait()
        for k in range(count):
            here, mine = lanes_at(k), slice(k * orbitals, (k + 1) * orbitals)
            high, rest = halves(buffer[0, mine, :])
            data_high[:orbitals, here] = high
            data_rest[:orbitals, here] = rest
            high, rest = halves(buffer[1, mine, :])
            other_high[:, here] = high
            other_rest[:, here] = rest
        other_high[:, width:] = jnp.zeros((orbitals, LANES), BF16)
        other_rest[:, width:] = jnp.zeros((orbitals, LANES), BF16)
        for k in range(count):
            entry, place = lists[wanted, k], jnp.int32(count)
            for l in range(count):
                place = jnp.where(entry == lists[1 - wanted, l], jnp.int32(l), place)
            here, there = lanes_at(k), lanes_at(place)
            data_high[orbitals:, here] = other_high[:, there]
            data_rest[orbitals:, here] = other_rest[:, there]
        note[...] = note_of(lambda k: lists[wanted, k].astype(jnp.int32), count)
        stores = [
            pltpu.make_async_copy(note, out_ref.at[pl.ds(rows, 8)], out_sems.at[0]),
            pltpu.make_async_copy(result, out_ref.at[pl.ds(0, rows)], out_sems.at[1]),
        ]
        stores[0].start()
        turn = jnp.concatenate(compact(jnp.concatenate([turn_ref[0], turn_ref[1]], axis=1), orbitals), axis=0)
        chunk = min(4, count)
        for first in range(0, count, chunk):
            here = lanes_at(first, chunk)
            value = stacked_dot(turn, (data_high[:, here], data_rest[:, here]), orbitals, NN)
            for j in range(chunk):
                k = first + j
                result[k * orbitals : (k + 1) * orbitals, :] = value[:, lanes_at(j)]
        stores[1].start()
        for copy in stores:
            copy.wait()


def swap(block, pairs):
    return lax.ppermute(block, "orb", both_ways(pairs))


def both_ways(pairs):
    return [pair for k in pairs for pair in ((k, k + 1), (k + 1, k))]


def shards(coeff, metric_coeff, tile_list, tile_atoms):
    groups, parts = lax.axis_size("orb"), lax.axis_size("ao")
    _, _, count, orbitals, lanes = coeff.shape
    rows, size, width = count * orbitals, 2 * orbitals, count * lanes
    keep = packed_rows(orbitals)[0]
    dma = pltpu.SemaphoreType.DMA
    inner = range(1, groups - 1, 2)
    direct = [k for k in inner if k % 4 != 3]
    across = [k for k in inner if k % 4 == 3]
    carried = jax.ShapeDtypeStruct((2, 2, size, width + lanes), BF16)

    def call(kernel, name, vmem, out_shape, scratch, *operands, specs=None, out_specs=None, cost=None):
        return pl.pallas_call(
            kernel,
            out_shape=out_shape,
            in_specs=specs or [HBM] * len(operands),
            out_specs=out_specs or [HBM] * len(out_shape),
            scratch_shapes=scratch,
            compiler_params=pltpu.CompilerParams(vmem_limit_bytes=vmem),
            cost_estimate=cost,
            name=name,
        )(*operands)

    def shaped(*shape):
        return jax.ShapeDtypeStruct(shape, F32)

    inputs = (tile_list, coeff.reshape(2, rows, lanes), metric_coeff.reshape(2, rows, lanes))
    inputs = tuple(pltpu.with_memory_space_constraint(array, pltpu.HBM) for array in inputs)
    tile_atoms = pltpu.with_memory_space_constraint(tile_atoms, pltpu.HBM)
    raw = swap(inputs[1], direct)
    for first_round in (True, False):
        final = not first_round
        loading = [
            pltpu.VMEM((2, 2, rows, lanes), F32),
            pltpu.SMEM((2, 1, count), jnp.int32) if first_round else pltpu.SMEM((2, 8, lanes), F32),
            dma((2, 3)),
        ]
        gradient, *split = call(
            functools.partial(gradient_kernel, first_round, count, orbitals, len(inputs)),
            "gradient",
            SOME_VMEM,
            (shaped(parts, keep, lanes), carried, carried),
            loading
            + [
                pltpu.VMEM(tile_atoms.shape, jnp.int32),
                dma,
                pltpu.VMEM((2, 2, size, width), BF16),
            ],
            tile_atoms,
            *inputs,
            out_specs=(VMEM,) * 3,
        )
        gathered = lax.all_to_all(gradient, "ao", 0, 0)
        packed, norms = call(
            norm_kernel,
            "norm",
            SOME_VMEM,
            (shaped(keep, lanes), shaped(groups, 8, lanes)),
            [],
            gathered,
            specs=[VMEM],
            out_specs=(VMEM, VMEM),
        )
        if first_round:
            norms, raw = lax.optimization_barrier((norms, raw))
        norms = lax.all_to_all(norms, "orb", 0, 0)
        squares = [pltpu.VMEM((size, 2 * lanes), F32)] * 2
        listing = [pltpu.SMEM((2, 1, count), jnp.int32), dma]
        turns = jax.ShapeDtypeStruct((2, size, size), BF16)
        kernel = functools.partial(rotation_kernel, first_round, count, orbitals, groups)
        if final:
            outs = call(
                kernel,
                "rotation",
                SOME_VMEM,
                (shaped(2, rows, lanes),) * 2,
                [pltpu.VMEM((2, 2, rows, lanes), F32), dma((2, 2)), *squares, pltpu.VMEM(turns.shape, BF16)],
                norms,
                packed,
                *split,
                specs=[VMEM] * 4,
            )
            return tuple(out.reshape(coeff.shape) for out in outs)
        odd_coeff, odd_metric, turn, turns = call(
            kernel,
            "rotation",
            SOME_VMEM,
            (shaped(rows + 8, lanes), shaped(rows, lanes), shaped(8 + size, lanes), turns),
            listing + squares,
            norms,
            packed,
            *split,
            inputs[0],
            specs=[VMEM] * 4 + [HBM],
            out_specs=[VMEM] * 4,
        )
        halfway = lax.ppermute(
            odd_coeff, "orb", [route for k in across for route in ((k, k + 4), (k + 1, k - 3))]
        )
        got_turn = swap(turn, direct)
        got_metric = swap(odd_metric, inner)
        turns, got_turn = lax.optimization_barrier((turns, got_turn))
        (even,) = call(
            functools.partial(later_kernel, count, orbitals),
            "later",
            SOME_VMEM,
            (shaped(2 * rows + 8, lanes),),
            listing,
            turns,
            *split,
            inputs[0],
            specs=[VMEM] * 3 + [HBM],
            out_specs=[VMEM],
        )
        got_even = swap(even, range(0, groups, 2))
        relayed = lax.ppermute(
            halfway, "orb", [route for k in across for route in ((k + 4, k + 1), (k - 3, k))]
        )
        half = pltpu.VMEM((orbitals, width + lanes), BF16)
        (rebuilt,) = call(
            functools.partial(crossing_kernel, count, orbitals),
            "crossing",
            SOME_VMEM,
            (shaped(rows + 8, lanes),),
            [
                pltpu.VMEM((2, rows, lanes), F32),
                pltpu.SMEM((8, lanes), F32),
                pltpu.VMEM((2, orbitals, lanes), F32),
                pltpu.VMEM((8, lanes), F32),
                pltpu.VMEM((rows, lanes), F32),
                dma((2, 3)),
                dma((2,)),
                pltpu.VMEM((size, width), BF16),
                pltpu.VMEM((size, width), BF16),
                half,
                half,
            ],
            raw,
            got_turn,
            cost=pl.CostEstimate(flops=2000 * orbitals * size * width, bytes_accessed=16 * rows * lanes, transcendentals=0),
        )
        inputs = (odd_coeff, odd_metric, got_even, got_metric, relayed, rebuilt)


def solution(mesh):
    blocks = P(None, "orb", "ao", None, None)
    return jax.shard_map(
        shards,
        mesh=mesh,
        in_specs=(blocks, blocks, P(None, "orb", "ao"), P()),
        out_specs=(blocks, blocks),
        check_vma=False,
    )
```

```python
import functools

import jax
import jax.numpy as jnp
from jax import lax
from jax.experimental import pallas as pl
from jax.experimental.pallas import tpu as pltpu
from jax.sharding import PartitionSpec as P

ATOMS = 8
LANES = 128
STEP_LENGTH = 3.0
EPSILON = 1e-12
CONVERGED = 1.2e-7
SOME_VMEM = 20_000_000

F32 = jnp.float32
BF16 = jnp.bfloat16
NT = (((1,), (1,)), ((), ()))
NN = (((1,), (0,)), ((), ()))
HBM = pl.BlockSpec(memory_space=pltpu.HBM)
VMEM = pl.BlockSpec(memory_space=pltpu.VMEM)


def halves(value):
    high = value.astype(BF16)
    return high, (value - high.astype(F32)).astype(BF16)


def dot(left, right, dims):
    return lax.dot_general(left, right, dims, preferred_element_type=F32)


def stacked_dot(left, right, rows, dims):
    wide = dot(left, right[0], dims)
    return wide[:rows] + (wide[rows:] + dot(left[:rows], right[1], dims))


def packed_rows(orbitals):
    pieces = -(-orbitals // (LANES - orbitals))
    tail = 2 * orbitals // (pieces + 1) // 8 * 8
    return 2 * orbitals - tail, tail, pieces


def pack(value, orbitals):
    keep, tail, pieces = packed_rows(orbitals)
    spare = LANES - orbitals
    lane = lax.broadcasted_iota(jnp.int32, (tail, LANES), 1)
    moved = [
        jnp.where(lane >= orbitals, pltpu.roll(value[keep:], (orbitals - i * spare) % LANES, 1), 0.0)
        for i in range(pieces)
    ]
    if keep > pieces * tail:
        moved.append(jnp.zeros((keep - pieces * tail, LANES), F32))
    return value[:keep] + jnp.concatenate(moved, axis=0)


def unpack(value, orbitals):
    keep, tail, pieces = packed_rows(orbitals)
    spare = LANES - orbitals
    lane = lax.broadcasted_iota(jnp.int32, (keep, LANES), 1)
    moved = jnp.where(lane >= orbitals, value, 0.0)
    last = sum(
        pltpu.roll(moved[i * tail : (i + 1) * tail], (i * spare - orbitals) % LANES, 1) for i in range(pieces)
    )
    return jnp.concatenate([jnp.where(lane < orbitals, value, 0.0), last], axis=0)


def crosses(position, last):
    return ((position % 4 == 3) & (position < last)) | ((position % 4 == 0) & (position > 0))


class Blocks:
    def __init__(self, first_round, refs, buffer, lists, sems, count, orbitals):
        self.count, self.orbitals, self.buffer, self.lists, self.sems = count, orbitals, buffer, lists, sems
        self.first_round, self.refs = first_round, refs

    def copy(self, slot, part, source):
        target = self.lists.at[slot] if part == 2 else self.buffer.at[slot, part]
        return pltpu.make_async_copy(source, target, self.sems.at[slot, part])

    def start(self):
        rows = self.count * self.orbitals
        if self.first_round:
            tile_list, coeff, metric = self.refs
            for slot in (1, 0):
                for part, source in ((2, tile_list), (0, coeff), (1, metric)):
                    self.copy(slot, part, source.at[slot]).start()
            return
        own_coeff, own_metric, even, odd_metric, relayed, rebuilt = self.refs
        position, last = lax.axis_index("orb"), lax.axis_size("orb") - 1
        odd = position % 2 == 1
        across = crosses(position, last)

        def begin(condition, slot, coeff, metric, metric_row):
            note_row = 2 * rows if metric_row else rows

            @pl.when(condition)
            def _():
                self.copy(slot, 2, coeff.at[pl.ds(note_row, 8)]).start()
                self.copy(slot, 0, coeff.at[pl.ds(0, rows)]).start()
                self.copy(slot, 1, metric.at[pl.ds(metric_row, rows)]).start()

        for slot, from_even, end in ((1, jnp.logical_not(odd), last), (0, odd, 0)):
            from_odd = jnp.logical_not(from_even) & (position != end)
            begin(from_even, slot, even, even, rows)
            begin(position == end, slot, own_coeff, own_metric, 0)
            begin(from_odd & across, slot, relayed, odd_metric, 0)
            begin(from_odd & jnp.logical_not(across), slot, rebuilt, odd_metric, 0)

    def wait(self, slot):
        for part in (2, 0, 1):
            if self.first_round:
                source = self.refs[0 if part == 2 else 1].at[slot]
            else:
                source = self.refs[0].at[pl.ds(0, 8 if part == 2 else self.count * self.orbitals)]
            self.copy(slot, part, source).wait()

    def tile(self, slot, k):
        return self.lists[slot, 0, k].astype(jnp.int32)

    def value(self, slot, c, k):
        return self.buffer[slot, c, k * self.orbitals : (k + 1) * self.orbitals, :]

    def wide(self, slot, c, k):
        return jnp.concatenate([self.value(slot, c, k), self.value(slot, c, k + 1)], axis=1)

    def place(self, slot, k):
        entry, place = self.tile(slot, k), jnp.int32(self.count)
        for l in range(self.count):
            place = jnp.where(entry == self.tile(1 - slot, l), jnp.int32(l), place)
        return place


def own_rows(slot, orbitals):
    return slice(slot * orbitals, (slot + 1) * orbitals)


def lanes_at(k, tiles=1):
    if isinstance(k, int):
        return slice(k * LANES, (k + tiles) * LANES)
    return pl.ds(pl.multiple_of(k * LANES, LANES), tiles * LANES)


def clear_spare(slot, blocks, arrays):
    for array in arrays:
        for c in range(2):
            array[slot, c, own_rows(slot, blocks.orbitals), blocks.count * LANES :] = jnp.zeros(
                (blocks.orbitals, LANES), BF16
            )


def carry(blocks, arrays):
    for slot in range(2):
        rows = own_rows(1 - slot, blocks.orbitals)
        for k in range(blocks.count):
            here, there = lanes_at(k), lanes_at(blocks.place(slot, k))
            for array in arrays:
                for c in range(2):
                    array[slot, c, rows, here] = array[1 - slot, c, rows, there]


def gradient_kernel(first_round, count, orbitals, sources, atoms_hbm, *refs):
    inputs, refs = refs[:sources], refs[sources:]
    out_ref, right_high, right_rest, buffer, lists, sems, atoms_ref, atoms_sem, left = refs
    blocks = Blocks(first_round, inputs, buffer, lists, sems, count, orbitals)
    atoms_copy = pltpu.make_async_copy(atoms_hbm, atoms_ref, atoms_sem)
    atoms_copy.start()
    blocks.start()
    width, gap = count * LANES, LANES - orbitals
    chunk = min(16, count)
    slots = lax.broadcasted_iota(jnp.int32, (ATOMS, LANES), 0)
    blank = jnp.zeros((ATOMS, LANES), F32)
    lane = lax.broadcasted_iota(jnp.int32, (orbitals, count * ATOMS), 1) // (2 * ATOMS)
    atoms_copy.wait()

    for slot in (1, 0):
        blocks.wait(slot)
        clear_spare(slot, blocks, (right_high, right_rest))
        rows = own_rows(slot, orbitals)
        member = []
        for k in range(count):
            one = (atoms_ref[pl.ds(blocks.tile(slot, k), 1), :] == slots).astype(F32)
            member.append(jnp.concatenate([blank, one] if k % 2 else [one, blank], axis=1))
        member = jnp.concatenate(member, axis=0).astype(BF16)
        member_wide = jnp.concatenate([member, member], axis=1)
        member_tall = jnp.concatenate([member, member], axis=0)

        for first in range(0, count, chunk):
            pairs = range(0, chunk, 2)
            coeffs = jnp.concatenate([blocks.wide(slot, 0, first + k) for k in pairs], axis=0)
            metric = jnp.concatenate([blocks.wide(slot, 1, first + k) for k in pairs], axis=0)
            charges = dot(jnp.concatenate(halves(coeffs * metric), axis=1), member_wide, NT)
            charges = jnp.concatenate(
                [
                    jnp.where(lane == first // 2 + j, charges[j * orbitals : (j + 1) * orbitals], 0.0)
                    for j in range(len(pairs))
                ],
                axis=0,
            )
            spread = dot(jnp.concatenate(halves(charges), axis=1), member_tall, NN)
            for c, value in enumerate((coeffs, metric)):
                weighted, plain = halves(value * spread), halves(value)
                for j, k in enumerate(pairs):
                    picked, here = slice(j * orbitals, (j + 1) * orbitals), lanes_at(first + k, 2)
                    left[slot, c, :orbitals, here] = weighted[0][picked]
                    left[slot, c, orbitals:, here] = weighted[1][picked]
                    right_high[slot, c, rows, here] = plain[0][picked]
                    right_rest[slot, c, rows, here] = plain[1][picked]


    carry(blocks, (right_high, right_rest))
    fill_lanes = jnp.zeros((2 * orbitals, gap), F32)
    fill_rows = jnp.zeros((gap, LANES), F32)
    products = []
    for slot in range(2):
        wide = sum(dot(right_high[slot, 1 - c, :, :width], left[slot, c], NT) for c in range(2))
        rest = sum(dot(right_rest[slot, 1 - c, :, :width], left[slot, c, :orbitals], NT) for c in range(2))
        value = jnp.concatenate([wide[:, :orbitals] + (wide[:, orbitals:] + rest), fill_lanes], axis=1)
        products.append(
            [jnp.concatenate([value[own_rows(i, orbitals)], fill_rows], axis=0) for i in range(2)]
        )
    (upper, upper_lower), (lower_upper, lower) = products
    row = lax.broadcasted_iota(jnp.int32, (LANES, LANES), 0)
    column = lax.broadcasted_iota(jnp.int32, (LANES, LANES), 1)
    diagonal = jnp.where(column > row, upper.T - upper, jnp.where(column < row, lower.T - lower, 0.0))
    cross = upper_lower.T - lower_upper
    packed = pack(jnp.concatenate([2.0 * diagonal[:orbitals], 2.0 * cross[:orbitals]], axis=0), orbitals)
    for z in range(out_ref.shape[0]):
        out_ref[z] = packed

def norm_kernel(parts_ref, packed_ref, norm_ref):
    packed = parts_ref[0]
    for z in range(1, parts_ref.shape[0]):
        packed = packed + parts_ref[z]
    packed_ref[...] = packed
    total = jnp.broadcast_to(2.0 * jnp.sum(packed * packed, keepdims=True), norm_ref.shape[1:])
    for g in range(norm_ref.shape[0]):
        norm_ref[g] = total


def compact(turn, orbitals):
    lane = lax.broadcasted_iota(jnp.int32, turn.shape, 1)
    turn = jnp.where(lane < LANES, turn, 0.0) + pltpu.roll(
        jnp.where(lane >= LANES, turn, 0.0), LANES + orbitals, 1
    )
    return halves(turn[:, : 2 * orbitals])


def later_slot(position):
    return jnp.where((position % 2 == 0) & (position != 0), 0, 1)


def note_of(tile, count):
    lane = lax.broadcasted_iota(jnp.int32, (8, LANES), 1)
    ids = jnp.zeros((8, LANES), jnp.int32)
    for k in range(count):
        ids = jnp.where(lane == k, tile(k), ids)
    return ids.astype(F32)


def apply(turn_ref, slot, c, data_high, data_rest, count, orbitals, put):
    chunk = min(4, count)
    for first in range(0, count, chunk):
        here = lanes_at(first, chunk)
        value = stacked_dot(
            turn_ref[slot], (data_high[slot, c, :, here], data_rest[slot, c, :, here]), orbitals, NN
        )
        for j in range(chunk):
            put(slice((first + j) * orbitals, (first + j + 1) * orbitals), value[:, lanes_at(j)])


def later_kernel(count, orbitals, turn_ref, data_high, data_rest, list_hbm, out_ref, lists, list_sem):
    rows = count * orbitals
    list_copy = pltpu.make_async_copy(list_hbm, lists, list_sem)
    list_copy.start()
    slot = later_slot(lax.axis_index("orb"))
    for c in range(2):

        def put(place, value, c=c):
            out_ref[c * rows + place.start : c * rows + place.stop, :] = value

        apply(turn_ref, slot, c, data_high, data_rest, count, orbitals, put)
    list_copy.wait()
    out_ref[2 * rows :] = note_of(lambda k: lists[slot, 0, k], count)


def rotation_kernel(first_round, count, orbitals, groups, *refs):
    norm_ref, packed_ref, data_high, data_rest = refs[:4]
    final = not first_round
    if first_round:
        list_hbm, odd_coeff, odd_metric, rows_ref, turn_ref, lists, list_sem, power_ref, total_ref = refs[4:]
        list_copy = pltpu.make_async_copy(list_hbm, lists, list_sem)
        list_copy.start()
    else:
        outs, (result, out_sems, power_ref, total_ref, turn_ref) = refs[4:6], refs[6:]
    size, wide, gap = 2 * orbitals, 2 * LANES, LANES - orbitals
    rows = count * orbitals

    squares = norm_ref[0]
    for g in range(1, groups):
        squares = squares + norm_ref[g]
    scale = (STEP_LENGTH / jnp.sqrt(squares / groups + EPSILON))[:1, :]
    row = lax.broadcasted_iota(jnp.int32, (LANES, LANES), 0)
    column = lax.broadcasted_iota(jnp.int32, (LANES, LANES), 1)
    fill = jnp.zeros((gap, LANES), F32)
    scaled = unpack(packed_ref[...], orbitals) * (-0.5 * scale)
    diagonal = jnp.concatenate([scaled[:orbitals], fill], axis=0)
    cross = jnp.concatenate([scaled[orbitals:], fill], axis=0)
    above = jnp.where(column > row, diagonal, 0.0)
    below = jnp.where(column < row, diagonal, 0.0)
    generator = jnp.concatenate(
        [
            jnp.concatenate([(above - above.T)[:orbitals], cross[:orbitals]], axis=1),
            jnp.concatenate([-cross.T[:orbitals], (below - below.T)[:orbitals]], axis=1),
        ],
        axis=0,
    )
    big_row = lax.broadcasted_iota(jnp.int32, (size, wide), 0)
    big_column = lax.broadcasted_iota(jnp.int32, (size, wide), 1)
    identity = (big_column == jnp.where(big_row < orbitals, big_row, big_row + gap)).astype(F32)

    def spaced(value):
        blank = jnp.zeros((gap, wide), value.dtype)
        return jnp.concatenate([value[:orbitals], blank, value[orbitals:], blank], axis=0)

    def times(left, right):
        high, rest = halves(right)
        return stacked_dot(
            jnp.concatenate(halves(left), axis=0), (spaced(high), spaced(rest)), left.shape[0], NN
        )

    square = -times(generator, generator)
    bound = jnp.sqrt(0.5 * jnp.sum(square * square, keepdims=True))
    centre = 1.0 + 0.5 * bound
    radius = 0.5 * bound / centre
    power_ref[...] = radius * identity - square * (1.0 / centre)
    total_ref[...] = identity + generator

    def more(radius):
        power, total = power_ref[...], total_ref[...]
        product = times(jnp.concatenate([total, power], axis=0), power)
        total_ref[...] = total + product[:size]
        power_ref[...] = product[size:]
        return radius * radius

    lax.while_loop(lambda radius: radius > CONVERGED, more, jnp.max(radius))
    turn = total_ref[...] * (2.0 / centre) - identity
    turn_high, turn_rest = compact(turn, orbitals)
    for slot in range(2):
        mine = own_rows(slot, orbitals)
        turn_ref[slot, :orbitals] = turn_high[mine]
        turn_ref[slot, orbitals:] = turn_rest[mine]

    if final:
        stores = []
        for slot in range(2):
            for c in range(2):

                def put(place, value, slot=slot, c=c):
                    result[slot, c, place, :] = value

                apply(turn_ref, slot, c, data_high, data_rest, count, orbitals, put)
                stores.append(
                    pltpu.make_async_copy(result.at[slot, c], outs[c].at[slot], out_sems.at[slot, c])
                )
                stores[-1].start()
        for copy in stores:
            copy.wait()
        return
    slot = 1 - later_slot(lax.axis_index("orb"))
    total_ref[...] = turn
    odd_rows = pl.ds(pl.multiple_of(slot * orbitals, 8), orbitals)
    rows_ref[8 : 8 + orbitals] = total_ref[odd_rows, :LANES]
    rows_ref[8 + orbitals :] = total_ref[odd_rows, LANES:]
    list_copy.wait()
    row = lax.broadcasted_iota(jnp.int32, (8, LANES), 0)
    notes = [note_of(lambda k, i=i: lists[i, 0, k], count) for i in range(2)]
    rows_ref[:8] = jnp.where(row == 0, notes[0], notes[1])
    odd_coeff[rows:] = jnp.where(slot == 0, notes[0], notes[1])
    for c, out_ref in enumerate((odd_coeff, odd_metric)):

        def put(place, value, out_ref=out_ref):
            out_ref[place, :] = value

        apply(turn_ref, slot, c, data_high, data_rest, count, orbitals, put)


def crossing_kernel(count, orbitals, raw_hbm, turn_hbm, out_ref, *refs):
    buffer, lists, turn_ref, note, result, sems, out_sems = refs[:7]
    data_high, data_rest, other_high, other_rest = refs[7:]
    position, last = lax.axis_index("orb"), lax.axis_size("orb") - 1
    rows, width = count * orbitals, count * LANES

    @pl.when(((position % 4 == 1) & (position < last)) | (position % 4 == 2))
    def _():
        wanted = position % 2
        loads = [pltpu.make_async_copy(turn_hbm.at[pl.ds(0, 8)], lists, sems.at[0, 0])]
        for i, block in enumerate((wanted, 1 - wanted)):
            first = pl.multiple_of(8 + block * orbitals, 8)
            loads.append(pltpu.make_async_copy(raw_hbm.at[block], buffer.at[i], sems.at[i, 1]))
            loads.append(
                pltpu.make_async_copy(turn_hbm.at[pl.ds(first, orbitals)], turn_ref.at[i], sems.at[i, 2])
            )
        for copy in loads:
            copy.start()
        for copy in loads:
            copy.wait()
        for k in range(count):
            here, mine = lanes_at(k), slice(k * orbitals, (k + 1) * orbitals)
            high, rest = halves(buffer[0, mine, :])
            data_high[:orbitals, here] = high
            data_rest[:orbitals, here] = rest
            high, rest = halves(buffer[1, mine, :])
            other_high[:, here] = high
            other_rest[:, here] = rest
        other_high[:, width:] = jnp.zeros((orbitals, LANES), BF16)
        other_rest[:, width:] = jnp.zeros((orbitals, LANES), BF16)
        for k in range(count):
            entry, place = lists[wanted, k], jnp.int32(count)
            for l in range(count):
                place = jnp.where(entry == lists[1 - wanted, l], jnp.int32(l), place)
            here, there = lanes_at(k), lanes_at(place)
            data_high[orbitals:, here] = other_high[:, there]
            data_rest[orbitals:, here] = other_rest[:, there]
        note[...] = note_of(lambda k: lists[wanted, k].astype(jnp.int32), count)
        stores = [
            pltpu.make_async_copy(note, out_ref.at[pl.ds(rows, 8)], out_sems.at[0]),
            pltpu.make_async_copy(result, out_ref.at[pl.ds(0, rows)], out_sems.at[1]),
        ]
        stores[0].start()
        turn = jnp.concatenate(compact(jnp.concatenate([turn_ref[0], turn_ref[1]], axis=1), orbitals), axis=0)
        chunk = min(4, count)
        for first in range(0, count, chunk):
            here = lanes_at(first, chunk)
            value = stacked_dot(turn, (data_high[:, here], data_rest[:, here]), orbitals, NN)
            for j in range(chunk):
                k = first + j
                result[k * orbitals : (k + 1) * orbitals, :] = value[:, lanes_at(j)]
        stores[1].start()
        for copy in stores:
            copy.wait()


def swap(block, pairs):
    return lax.ppermute(block, "orb", both_ways(pairs))


def both_ways(pairs):
    return [pair for k in pairs for pair in ((k, k + 1), (k + 1, k))]


def shards(coeff, metric_coeff, tile_list, tile_atoms):
    groups, parts = lax.axis_size("orb"), lax.axis_size("ao")
    _, _, count, orbitals, lanes = coeff.shape
    rows, size, width = count * orbitals, 2 * orbitals, count * lanes
    keep = packed_rows(orbitals)[0]
    dma = pltpu.SemaphoreType.DMA
    inner = range(1, groups - 1, 2)
    direct = [k for k in inner if k % 4 != 3]
    across = [k for k in inner if k % 4 == 3]
    carried = jax.ShapeDtypeStruct((2, 2, size, width + lanes), BF16)

    def call(kernel, name, vmem, out_shape, scratch, *operands, specs=None, out_specs=None, cost=None):
        return pl.pallas_call(
            kernel,
            out_shape=out_shape,
            in_specs=specs or [HBM] * len(operands),
            out_specs=out_specs or [HBM] * len(out_shape),
            scratch_shapes=scratch,
            compiler_params=pltpu.CompilerParams(vmem_limit_bytes=vmem),
            cost_estimate=cost,
            name=name,
        )(*operands)

    def shaped(*shape):
        return jax.ShapeDtypeStruct(shape, F32)

    inputs = (tile_list, coeff.reshape(2, rows, lanes), metric_coeff.reshape(2, rows, lanes))
    inputs = tuple(pltpu.with_memory_space_constraint(array, pltpu.HBM) for array in inputs)
    tile_atoms = pltpu.with_memory_space_constraint(tile_atoms, pltpu.HBM)
    raw = swap(inputs[1], direct)
    for first_round in (True, False):
        final = not first_round
        loading = [
            pltpu.VMEM((2, 2, rows, lanes), F32),
            pltpu.SMEM((2, 1, count), jnp.int32) if first_round else pltpu.SMEM((2, 8, lanes), F32),
            dma((2, 3)),
        ]
        gradient, *split = call(
            functools.partial(gradient_kernel, first_round, count, orbitals, len(inputs)),
            "gradient",
            SOME_VMEM,
            (shaped(parts, keep, lanes), carried, carried),
            loading
            + [
                pltpu.VMEM(tile_atoms.shape, jnp.int32),
                dma,
                pltpu.VMEM((2, 2, size, width), BF16),
            ],
            tile_atoms,
            *inputs,
            out_specs=(VMEM,) * 3,
        )
        gathered = lax.all_to_all(gradient, "ao", 0, 0)
        packed, norms = call(
            norm_kernel,
            "norm",
            SOME_VMEM,
            (shaped(keep, lanes), shaped(groups, 8, lanes)),
            [],
            gathered,
            specs=[VMEM],
            out_specs=(VMEM, VMEM),
        )
        if first_round:
            norms, raw = lax.optimization_barrier((norms, raw))
        norms = lax.all_to_all(norms, "orb", 0, 0)
        squares = [pltpu.VMEM((size, 2 * lanes), F32)] * 2
        listing = [pltpu.SMEM((2, 1, count), jnp.int32), dma]
        turns = jax.ShapeDtypeStruct((2, size, size), BF16)
        kernel = functools.partial(rotation_kernel, first_round, count, orbitals, groups)
        if final:
            outs = call(
                kernel,
                "rotation",
                SOME_VMEM,
                (shaped(2, rows, lanes),) * 2,
                [pltpu.VMEM((2, 2, rows, lanes), F32), dma((2, 2)), *squares, pltpu.VMEM(turns.shape, BF16)],
                norms,
                packed,
                *split,
                specs=[VMEM] * 4,
            )
            return tuple(out.reshape(coeff.shape) for out in outs)
        odd_coeff, odd_metric, turn, turns = call(
            kernel,
            "rotation",
            SOME_VMEM,
            (shaped(rows + 8, lanes), shaped(rows, lanes), shaped(8 + size, lanes), turns),
            listing + squares,
            norms,
            packed,
            *split,
            inputs[0],
            specs=[VMEM] * 4 + [HBM],
            out_specs=[VMEM] * 4,
        )
        halfway = lax.ppermute(
            odd_coeff, "orb", [route for k in across for route in ((k, k + 4), (k + 1, k - 3))]
        )
        got_turn = swap(turn, direct)
        got_metric = swap(odd_metric, inner)
        turns, got_turn = lax.optimization_barrier((turns, got_turn))
        (even,) = call(
            functools.partial(later_kernel, count, orbitals),
            "later",
            SOME_VMEM,
            (shaped(2 * rows + 8, lanes),),
            listing,
            turns,
            *split,
            inputs[0],
            specs=[VMEM] * 3 + [HBM],
            out_specs=[VMEM],
        )
        got_even = swap(even, range(0, groups, 2))
        relayed = lax.ppermute(
            halfway, "orb", [route for k in across for route in ((k + 4, k + 1), (k - 3, k))]
        )
        half = pltpu.VMEM((orbitals, width + lanes), BF16)
        (rebuilt,) = call(
            functools.partial(crossing_kernel, count, orbitals),
            "crossing",
            SOME_VMEM,
            (shaped(rows + 8, lanes),),
            [
                pltpu.VMEM((2, rows, lanes), F32),
                pltpu.SMEM((8, lanes), F32),
                pltpu.VMEM((2, orbitals, lanes), F32),
                pltpu.VMEM((8, lanes), F32),
                pltpu.VMEM((rows, lanes), F32),
                dma((2, 3)),
                dma((2,)),
                pltpu.VMEM((size, width), BF16),
                pltpu.VMEM((size, width), BF16),
                half,
                half,
            ],
            raw,
            got_turn,
            cost=pl.CostEstimate(flops=2000 * orbitals * size * width, bytes_accessed=16 * rows * lanes, transcendentals=0),
        )
        inputs = (odd_coeff, odd_metric, got_even, got_metric, relayed, rebuilt)


def solution(mesh):
    blocks = P(None, "orb", "ao", None, None)
    return jax.shard_map(
        shards,
        mesh=mesh,
        in_specs=(blocks, blocks, P(None, "orb", "ao"), P()),
        out_specs=(blocks, blocks),
        check_vma=False,
    )
```
